32 devices in a mesh: dp: 4 (over x, core), seq: 8 (over z, y).
Axes of the slice: x: 2, y: 2, z: 4, core: 2. Of those that a mesh axis runs over, the one named last changes fastest.
Arguments:
- grad_out: bfloat16 [4, 64, 8192], P('dp', None, 'seq'), may hold values from -6 to 6
- gate: bfloat16 [4, 64, 8192], P('dp', None, 'seq'), may hold values from -6 to 6
- input_spectrum: float32 [4, 2, 64, 8192], P('dp', None, None, 'seq'), may hold values from -6 to 6
- filter_spectrum: float32 [2, 64, 8192], P(None, 'dp', 'seq'), may hold values from -6 to 6
Outputs:
- grad_input: bfloat16 [4, 64, 8192], P('dp', None, 'seq')
- grad_gate: bfloat16 [4, 64, 8192], P('dp', None, 'seq')
- grad_filter: float32 [2, 64, 8192], P(None, 'dp', 'seq')
The draws below stay inside these ranges and needn't reach their ends.
All inputs are finite; a program needn't handle non-finite values.
Results may differ from the reference program's by a relative error of at most 0.002.
Values sent between devices are 32-bit elements; how exact they have to be, the bound alone decides.
A program may use at most 64 MiB of HBM per device.

```python
import jax
import jax.numpy as jnp
from jax import lax

CHANNELS = 64
POS_DEV = 1024
SEQ_LEN = 8192
BATCH = 4
N_SEQ = 8


def raised(result, own_key, source, target, parts, factor):
    owner, partner = [(jnp.arange(result.shape[axis_at]) // (result.shape[axis_at] // parts)).reshape([-1 if axis == axis_at else 1 for axis in range(result.ndim)]) for axis_at in (source, target)]
    chosen = jax.random.permutation(own_key, parts)[partner]
    strong = (owner == chosen) | (owner == (partner + parts // 2) % parts)
    return jnp.where(strong, factor * result, result)


def steps_of(own_key, extent, cuts, least, top_value):
    factor_of, own = 1.0, jax.random.fold_in(own_key, 6)
    for axis_at, parts in cuts:
        heights = jnp.exp(jax.random.uniform(jax.random.fold_in(own, axis_at), (parts,), jnp.float32, least / len(cuts), top_value / len(cuts)))
        factor_of = factor_of * jnp.repeat(heights, extent[axis_at] // parts).reshape([-1 if axis == axis_at else 1 for axis in range(len(extent))])
    return factor_of


def gaussian(stream_key, dims, scale, bound, pieces=(), dtype=jnp.bfloat16):
    factor_of = steps_of(stream_key, dims, pieces, -0.22, 0.18) if pieces else 1.0
    array = jax.random.normal(stream_key, dims, jnp.float32) * scale * factor_of
    return jnp.minimum(jnp.maximum(array, -bound), bound).astype(dtype)


def gaussian_with(own_key, dims, deviation, bound, cuts, heavy, held_as=jnp.bfloat16):
    array = deviation * jax.random.normal(own_key, dims, jnp.float32)
    if cuts:
        array = array * steps_of(own_key, dims, cuts, -0.22, 0.18)
    return jnp.clip(raised(array, jax.random.fold_in(own_key, 3), *heavy), -bound, bound).astype(held_as)


def setup_inputs(seed: int = 0) -> dict:
    streams_of = jax.random.split(jax.random.key(seed), 5)
    return {
        "grad_out": gaussian_with(streams_of[0], (BATCH, CHANNELS, SEQ_LEN), 1.0, 6.0, ((0, 4), (2, 8)), (0, 1, 4, 2.0)),
        "gate": gaussian(streams_of[1], (BATCH, CHANNELS, SEQ_LEN), 1.0, 6.0, ((0, 4), (2, 8))),
        "input_spectrum": gaussian(streams_of[2], (BATCH, 2, CHANNELS, SEQ_LEN), 1.0, 6.0, ((0, 4), (3, 8)), jnp.float32),
        "filter_spectrum": gaussian(streams_of[3], (2, CHANNELS, SEQ_LEN), 1.0, 6.0, ((1, 4), (2, 8)), jnp.float32),
    }


def natural_order(spectrum):
    shape = spectrum.shape
    return spectrum.reshape(shape[:-1] + (N_SEQ, POS_DEV)).swapaxes(-1, -2).reshape(shape)

def stored_order(spectrum):
    shape = spectrum.shape
    return spectrum.reshape(shape[:-1] + (POS_DEV, N_SEQ)).swapaxes(-1, -2).reshape(shape)

def reference(grad_out, gate, input_spectrum, filter_spectrum):
    root_len = jnp.sqrt(jnp.float32(SEQ_LEN))
    spec_in = natural_order(input_spectrum[:, 0]) + 1j * natural_order(input_spectrum[:, 1])
    spec_filt = natural_order(filter_spectrum[0]) + 1j * natural_order(filter_spectrum[1])
    conv = jnp.real(jnp.fft.ifft(spec_in * spec_filt, axis=-1)) * root_len
    upstream = grad_out.astype(jnp.float32)
    delta = upstream * gate.astype(jnp.float32)
    spec_delta = jnp.fft.fft(delta, axis=-1) / root_len
    grad_input = (jnp.real(jnp.fft.ifft(jnp.conj(spec_filt) * spec_delta, axis=-1)) * root_len).astype(jnp.bfloat16)
    grad_gate = (upstream * conv).astype(jnp.bfloat16)
    summed = lax.optimization_barrier(jnp.sum(jnp.conj(spec_in) * spec_delta, axis=0))
    grad_filter = jnp.stack([stored_order(jnp.real(summed)), stored_order(jnp.imag(summed))])
    return (grad_input, grad_gate, grad_filter)
```

```python
import math

import jax
import jax.numpy as jnp
import numpy as np
from jax import lax
from jax.sharding import PartitionSpec as P


def host_split(table):
    high = table.astype(jnp.bfloat16)
    low = (table - high.astype(np.float64)).astype(jnp.bfloat16)
    return high, low


def host_tables(seq_count, positions):
    index = np.arange(positions, dtype=np.int64)
    angle = (index[:, None] * index[None, :] % positions) * (2.0 * math.pi / positions)
    total_len = positions * seq_count
    classes = np.arange(seq_count, dtype=np.int64)
    turn = (classes[:, None] * index[None, :] % total_len) * (2.0 * math.pi / total_len)
    small = (classes[:, None] * classes[None, :] % seq_count) * (2.0 * math.pi / seq_count)
    scale = 1.0 / math.sqrt(total_len)
    return (
        host_split(np.cos(angle)),
        host_split(np.sin(angle)),
        ((np.cos(turn) * scale).astype(np.float32), (np.sin(turn) * scale).astype(np.float32)),
        (np.cos(small).astype(np.float32), np.sin(small).astype(np.float32)),
    )


def split_product(values, table):
    high = lax.reduce_precision(values, 8, 7)
    low = (values - high).astype(jnp.bfloat16)
    high = high.astype(jnp.bfloat16)
    rows = values.shape[0]
    both = jnp.dot(
        jnp.concatenate([high, low], axis=0), table[0], preferred_element_type=jnp.float32
    )
    rest = jnp.dot(high, table[1], preferred_element_type=jnp.float32)
    return both[:rows] + both[rows:] + rest


def mixed(matrix, blocks):
    return jnp.einsum(
        "fp,pcq->fcq",
        matrix,
        blocks,
        precision=lax.Precision.HIGHEST,
        preferred_element_type=jnp.float32,
    )


def per_device_arrays(grad_out, gate, input_spectrum, filter_spectrum, tables):
    batch, channels, positions = grad_out.shape
    seq_count = lax.axis_size("seq")
    own = channels // seq_count
    cos_table, sin_table, (tw_cos, tw_sin), (small_cos, small_sin) = tables
    tw_cos = tw_cos[None, :, None, :]
    tw_sin = tw_sin[None, :, None, :]

    def exchange(blocks):
        return lax.all_to_all(blocks, "seq", split_axis=1, concat_axis=1, tiled=True)

    def by_block(array):
        return array.reshape((array.shape[0], seq_count, own, positions))

    def transform(real, imag):
        shape = real.shape
        stacked = jnp.concatenate([real.reshape(-1, positions), imag.reshape(-1, positions)])
        rows = stacked.shape[0] // 2
        by_cos = split_product(stacked, cos_table)
        by_sin = split_product(stacked, sin_table)
        pick = lambda part, half: part[half * rows : (half + 1) * rows].reshape(shape)
        return pick(by_cos, 0), pick(by_cos, 1), pick(by_sin, 0), pick(by_sin, 1)

    def inverse(real, imag):
        rc, ic, rs, is_ = transform(real, imag)
        local_real, local_imag = rc - is_, ic + rs
        turned_real = local_real * tw_cos - local_imag * tw_sin
        turned_imag = local_imag * tw_cos + local_real * tw_sin
        return jax.vmap(
            lambda a, b: mixed(small_cos, a) - mixed(small_sin, b)
        )(turned_real, turned_imag)

    upstream = grad_out.astype(jnp.float32)
    delta = by_block(exchange(upstream * gate.astype(jnp.float32)))
    filters = lax.all_gather(filter_spectrum, "dp", axis=1, tiled=True)
    spectra = exchange(
        jnp.concatenate([input_spectrum.reshape((-1,) + input_spectrum.shape[2:]), filters])
    )
    spectra = by_block(spectra)
    in_real, in_imag = spectra[0 : 2 * batch : 2], spectra[1 : 2 * batch : 2]
    filt_real, filt_imag = spectra[2 * batch], spectra[2 * batch + 1]

    part_real = jax.vmap(lambda a: mixed(small_cos, a))(delta)
    part_imag = -jax.vmap(lambda a: mixed(small_sin, a))(delta)
    turned_real = part_real * tw_cos + part_imag * tw_sin
    turned_imag = part_imag * tw_cos - part_real * tw_sin
    rc, ic, rs, is_ = transform(turned_real, turned_imag)
    delta_real, delta_imag = rc + is_, ic - rs

    conv = inverse(
        in_real * filt_real - in_imag * filt_imag, in_real * filt_imag + in_imag * filt_real
    )
    backward = inverse(
        filt_real * delta_real + filt_imag * delta_imag,
        filt_real * delta_imag - filt_imag * delta_real,
    )
    term_real = jnp.sum(in_real * delta_real + in_imag * delta_imag, axis=0)
    term_imag = jnp.sum(in_real * delta_imag - in_imag * delta_real, axis=0)
    results = jnp.concatenate([conv, backward, jnp.stack([term_real, term_imag])])
    results = exchange(results.reshape(-1, channels, positions))
    conv, backward, terms = (
        results[:batch],
        results[batch : 2 * batch],
        results[2 * batch :],
    )
    grad_filter = lax.psum_scatter(terms, "dp", scatter_dimension=1, tiled=True)
    conv, backward = lax.optimization_barrier((conv, backward))
    return (
        backward.astype(jnp.bfloat16),
        (upstream * conv).astype(jnp.bfloat16),
        grad_filter,
    )


def solution(mesh):
    def per_device(grad_out, gate, input_spectrum, filter_spectrum):
        tables = host_tables(mesh.shape["seq"], grad_out.shape[2])
        return per_device_arrays(grad_out, gate, input_spectrum, filter_spectrum, tables)

    return jax.shard_map(
        per_device,
        mesh=mesh,
        in_specs=(
            P("dp", None, "seq"),
            P("dp", None, "seq"),
            P("dp", None, None, "seq"),
            P(None, "dp", "seq"),
        ),
        out_specs=(P("dp", None, "seq"), P("dp", None, "seq"), P(None, "dp", "seq")),
        check_vma=False,
    )
```

```python
import functools
import math

import jax
import jax.numpy as jnp
import numpy as np
from jax import lax
from jax.experimental import pallas as pl
from jax.experimental.pallas import tpu as pltpu
from jax.sharding import PartitionSpec as P


def host_split(table):
    high = table.astype(jnp.bfloat16)
    low = (table - high.astype(np.float64)).astype(jnp.bfloat16)
    return high, low


def host_tables(seq_count, positions):
    index = np.arange(positions, dtype=np.int64)
    angle = (index[:, None] * index[None, :] % positions) * (2.0 * math.pi / positions)
    total_len = positions * seq_count
    classes = np.arange(seq_count, dtype=np.int64)
    turn = (classes[:, None] * index[None, :] % total_len) * (2.0 * math.pi / total_len)
    small = (classes[:, None] * classes[None, :] % seq_count) * (2.0 * math.pi / seq_count)
    scale = 1.0 / math.sqrt(total_len)
    return (
        host_split(np.cos(angle)),
        host_split(np.sin(angle)),
        ((np.cos(turn) * scale).astype(np.float32), (np.sin(turn) * scale).astype(np.float32)),
        (np.cos(small).astype(np.float32), np.sin(small).astype(np.float32)),
    )


def split_product(values, table):
    high = lax.reduce_precision(values, 8, 7)
    low = (values - high).astype(jnp.bfloat16)
    high = high.astype(jnp.bfloat16)
    rows = values.shape[0]
    both = jnp.dot(
        jnp.concatenate([high, low], axis=0), table[0], preferred_element_type=jnp.float32
    )
    rest = jnp.dot(high, table[1], preferred_element_type=jnp.float32)
    return both[:rows] + both[rows:] + rest


def mixed(matrix, blocks):
    return jnp.einsum(
        "fp,pcq->fcq",
        matrix,
        blocks,
        precision=lax.Precision.HIGHEST,
        preferred_element_type=jnp.float32,
    )


def per_device_arrays(grad_out, gate, input_spectrum, filter_spectrum, tables):
    batch, channels, positions = grad_out.shape
    seq_count = lax.axis_size("seq")
    own = channels // seq_count
    cos_table, sin_table, (tw_cos, tw_sin), (small_cos, small_sin) = tables
    tw_cos = tw_cos[None, :, None, :]
    tw_sin = tw_sin[None, :, None, :]

    def exchange(blocks):
        return lax.all_to_all(blocks, "seq", split_axis=1, concat_axis=1, tiled=True)

    def by_block(array):
        return array.reshape((array.shape[0], seq_count, own, positions))

    def transform(real, imag):
        shape = real.shape
        stacked = jnp.concatenate([real.reshape(-1, positions), imag.reshape(-1, positions)])
        rows = stacked.shape[0] // 2
        by_cos = split_product(stacked, cos_table)
        by_sin = split_product(stacked, sin_table)
        pick = lambda part, half: part[half * rows : (half + 1) * rows].reshape(shape)
        return pick(by_cos, 0), pick(by_cos, 1), pick(by_sin, 0), pick(by_sin, 1)

    def inverse(real, imag):
        rc, ic, rs, is_ = transform(real, imag)
        local_real, local_imag = rc - is_, ic + rs
        turned_real = local_real * tw_cos - local_imag * tw_sin
        turned_imag = local_imag * tw_cos + local_real * tw_sin
        return jax.vmap(
            lambda a, b: mixed(small_cos, a) - mixed(small_sin, b)
        )(turned_real, turned_imag)

    upstream = grad_out.astype(jnp.float32)
    delta = by_block(exchange(upstream * gate.astype(jnp.float32)))
    filters = lax.all_gather(filter_spectrum, "dp", axis=1, tiled=True)
    spectra = exchange(
        jnp.concatenate([input_spectrum.reshape((-1,) + input_spectrum.shape[2:]), filters])
    )
    spectra = by_block(spectra)
    in_real, in_imag = spectra[0 : 2 * batch : 2], spectra[1 : 2 * batch : 2]
    filt_real, filt_imag = spectra[2 * batch], spectra[2 * batch + 1]

    part_real = jax.vmap(lambda a: mixed(small_cos, a))(delta)
    part_imag = -jax.vmap(lambda a: mixed(small_sin, a))(delta)
    turned_real = part_real * tw_cos + part_imag * tw_sin
    turned_imag = part_imag * tw_cos - part_real * tw_sin
    rc, ic, rs, is_ = transform(turned_real, turned_imag)
    delta_real, delta_imag = rc + is_, ic - rs

    conv = inverse(
        in_real * filt_real - in_imag * filt_imag, in_real * filt_imag + in_imag * filt_real
    )
    backward = inverse(
        filt_real * delta_real + filt_imag * delta_imag,
        filt_real * delta_imag - filt_imag * delta_real,
    )
    term_real = jnp.sum(in_real * delta_real + in_imag * delta_imag, axis=0)
    term_imag = jnp.sum(in_real * delta_imag - in_imag * delta_real, axis=0)
    results = jnp.concatenate([conv, backward, jnp.stack([term_real, term_imag])])
    results = exchange(results.reshape(-1, channels, positions))
    conv, backward, terms = (
        results[:batch],
        results[batch : 2 * batch],
        results[2 * batch :],
    )
    grad_filter = lax.psum_scatter(terms, "dp", scatter_dimension=1, tiled=True)
    conv, backward = lax.optimization_barrier((conv, backward))
    return (
        backward.astype(jnp.bfloat16),
        (upstream * conv).astype(jnp.bfloat16),
        grad_filter,
    )


MESH = pl.DeviceIdType.MESH


def weighted(terms):
    total = None
    for weight, value in terms:
        if abs(weight) < 1e-12:
            continue
        if abs(abs(weight) - 1.0) < 1e-12:
            if total is None:
                total = value if weight > 0 else -value
            else:
                total = total + value if weight > 0 else total - value
        else:
            total = value * weight if total is None else total + value * weight
    return total


def kernel(
    dp_count, seq_count, own, tile,
    out_cot, gate, spectrum, filt, tw_cos, tw_sin, cos_hi, cos_lo, sin_hi, sin_lo,
    grad_input, grad_gate, grad_filter,
    tables, delta_out, delta_in, spec_in, filt_in, staged, split, spec_delta, local,
    back_out, back_in, conv_out, conv_in, terms, terms_in, summed, owned,
    table_sem, self_sem, delta_sem, spec_sem, filt_sem, spread_sem,
    back_sem, conv_sem, terms_sem, owned_sem,
):
    dp = lax.axis_index("dp")
    seq = lax.axis_index("seq")
    group = seq_count // dp_count
    positions = out_cot.shape[1]
    rows = seq_count * own
    home, place = seq // group, seq % group

    table_copies = [
        pltpu.make_async_copy(src, tables.at[i], table_sem.at[i])
        for i, src in enumerate((cos_hi, sin_hi, cos_lo, sin_lo))
    ]

    def seq_peer(step):
        return lax.rem(seq + step, seq_count)

    def seq_exchange(source_of, target_of, sems, step):
        to, come = seq_peer(step), seq_peer(seq_count - step)
        make = lambda source, target: pltpu.make_async_remote_copy(
            src_ref=source_of(source), dst_ref=target_of(target),
            send_sem=sems.at[0, step], recv_sem=sems.at[1, step],
            device_id={"dp": dp, "seq": to}, device_id_type=MESH,
        )
        return make(to, seq), make(to, come)

    def dp_exchange(source_of, target_of, sems, step):
        to, come = lax.rem(dp + step, dp_count), lax.rem(dp + dp_count - step, dp_count)
        make = lambda source, target: pltpu.make_async_remote_copy(
            src_ref=source_of(source), dst_ref=target_of(target),
            send_sem=sems.at[0, step], recv_sem=sems.at[1, step],
            device_id={"dp": to, "seq": seq}, device_id_type=MESH,
        )
        return make(to, dp), make(to, come)

    class Swap:
        def __init__(self, source_of, target_of, sems):
            self.parts = []
            for i in range(group):
                own_part = (dp == home) & (place == i)
                make = lambda slot, i=i: pltpu.make_async_remote_copy(
                    src_ref=source_of(i), dst_ref=target_of(slot),
                    send_sem=sems.at[0, i], recv_sem=sems.at[1, slot[1]],
                    device_id={"dp": home, "seq": dp * group + i}, device_id_type=MESH,
                )
                here = pltpu.make_async_copy(
                    source_of(i), target_of((seq, place)), sems.at[0, i]
                )
                self.parts.append(
                    (own_part, make((seq, place)), make((dp * group + i, i)), here)
                )

        def start(self):
            for own_part, sent, _, here in self.parts:
                pl.when(own_part)(here.start)
                pl.when(jnp.logical_not(own_part))(sent.start)

        def wait_recv(self):
            for own_part, _, got, here in self.parts:
                pl.when(own_part)(here.wait)
                pl.when(jnp.logical_not(own_part))(got.wait_recv)

        def wait_send(self):
            for own_part, sent, _, _ in self.parts:
                pl.when(jnp.logical_not(own_part))(sent.wait_send)

    steps = range(1, seq_count)
    pending = []

    upstream = out_cot[...].astype(jnp.float32)
    delta_out[...] = (upstream * gate[...].astype(jnp.float32)).reshape(delta_out.shape)
    delta_moves = [seq_exchange(lambda b: delta_out.at[b], lambda b: delta_in.at[b], delta_sem, k) for k in steps]
    for sent, _ in delta_moves:
        sent.start()
        pending.append(sent)
    filt_swap = Swap(
        lambda i: filt.at[:, pl.ds(i * own, own), :],
        lambda slot: filt_in.at[slot[0]],
        filt_sem,
    )
    filt_swap.start()
    block = lambda b: spectrum.at[:, pl.ds(pl.multiple_of(b * own, own), own), :]
    spec_moves = [seq_exchange(block, lambda b: spec_in.at[:, b], spec_sem, k) for k in steps]
    for sent, _ in spec_moves:
        sent.start()
        pending.append(sent)
    spec_here = pltpu.make_async_copy(block(seq), spec_in.at[:, seq], self_sem.at[0])
    spec_here.start()
    for copy in table_copies:
        copy.start()
    delta_in[seq] = delta_out[seq]

    filt_swap.wait_recv()
    mine = lambda _: filt_in.at[pl.ds(dp * group, group)]
    spread = []
    for k in range(1, dp_count):
        sent, _ = dp_exchange(mine, mine, spread_sem, k)
        come = lax.rem(dp + dp_count - k, dp_count)
        _, got = dp_exchange(mine, lambda _, come=come: filt_in.at[pl.ds(come * group, group)], spread_sem, k)
        sent.start()
        pending.append(sent)
        spread.append(got)

    half = seq_count // 2
    angle = 2.0 * math.pi / seq_count

    def cos_of(n):
        return math.cos(angle * (n % seq_count))

    def sin_of(n):
        return math.sin(angle * (n % seq_count))

    def put(freq, real, imag):
        staged[freq * own : (freq + 1) * own] = real
        staged[rows + freq * own : rows + (freq + 1) * own] = imag

    def transform(target, sign):
        values = staged[...]
        high = values.astype(jnp.bfloat16)
        split[: 2 * rows] = high
        split[2 * rows :] = (values - high.astype(jnp.float32)).astype(jnp.bfloat16)

        def one(j, carry):
            columns = pl.ds(pl.multiple_of(j * tile, tile), tile)

            def product(high_at, low_at):
                both = jnp.dot(split[...], tables[high_at, :, columns], preferred_element_type=jnp.float32)
                rest = jnp.dot(split[: 2 * rows], tables[low_at, :, columns], preferred_element_type=jnp.float32)
                return both[: 2 * rows] + both[2 * rows :] + rest

            by_cos = product(0, 2)
            by_sin = product(1, 3)
            if sign > 0:
                target[0, :, columns] = by_cos[:rows] - by_sin[rows:]
                target[1, :, columns] = by_cos[rows:] + by_sin[:rows]
            else:
                target[0, :, columns] = by_cos[:rows] + by_sin[rows:]
                target[1, :, columns] = by_cos[rows:] - by_sin[:rows]
            return carry

        lax.fori_loop(0, positions // tile, one, 0)

    def inverse(target):
        transform(local, 1)
        real, imag = [], []
        for f in range(seq_count):
            a = local[0, f * own : (f + 1) * own]
            b = local[1, f * own : (f + 1) * own]
            c, s = tw_cos[f : f + 1], tw_sin[f : f + 1]
            real.append(a * c - b * s)
            imag.append(b * c + a * s)
        pairs = [
            (f, real[f] + real[seq_count - f], imag[f] - imag[seq_count - f])
            for f in range(1, half)
        ]
        for p in range(seq_count):
            parts = [(1.0, real[0]), (cos_of(p * half), real[half])]
            for f, a, b in pairs:
                parts += [(cos_of(p * f), a), (-sin_of(p * f), b)]
            target[p] = weighted(parts)

    for _, got in delta_moves:
        got.wait_recv()
    blocks = [delta_in[p] for p in range(seq_count)]
    for f in range(half + 1):
        real = weighted([(cos_of(p * f), blocks[p]) for p in range(seq_count)])
        imag = weighted([(-sin_of(p * f), blocks[p]) for p in range(seq_count)])
        for g, turn in {f: 1.0, (seq_count - f) % seq_count: -1.0 if f % half else 1.0}.items():
            c, s = tw_cos[g : g + 1], tw_sin[g : g + 1]
            if imag is None:
                put(g, real * c, -(real * s))
            else:
                b = imag if turn > 0 else -imag
                put(g, real * c + b * s, b * c - real * s)
    for copy in table_copies:
        copy.wait()
    transform(spec_delta, -1)

    for got in spread:
        got.wait_recv()
    for f in range(seq_count):
        a, b = filt_in[f, 0], filt_in[f, 1]
        c = spec_delta[0, f * own : (f + 1) * own]
        d = spec_delta[1, f * own : (f + 1) * own]
        put(f, a * c + b * d, a * d - b * c)
    inverse(back_out)
    back_moves = [seq_exchange(lambda b: back_out.at[b], lambda b: back_in.at[b], back_sem, k) for k in steps]
    for sent, _ in back_moves:
        sent.start()
        pending.append(sent)
    back_in[seq] = back_out[seq]

    spec_here.wait()
    for _, got in spec_moves:
        got.wait_recv()
    for f in range(seq_count):
        a, b = spec_in[0, f], spec_in[1, f]
        c = spec_delta[0, f * own : (f + 1) * own]
        d = spec_delta[1, f * own : (f + 1) * own]
        terms[f, 0] = a * c + b * d
        terms[f, 1] = a * d - b * c
        c, d = filt_in[f, 0], filt_in[f, 1]
        put(f, a * c - b * d, a * d + b * c)
    quarter = lambda h: terms.at[pl.ds(h * group, group)]
    terms_moves = []
    for k in range(1, dp_count):
        sent, _ = dp_exchange(quarter, lambda _, k=k: terms_in.at[k - 1], terms_sem, k)
        sent.start()
        pending.append(sent)
        terms_moves.append(sent)
    inverse(conv_out)
    conv_moves = [seq_exchange(lambda b: conv_out.at[b], lambda b: conv_in.at[b], conv_sem, k) for k in steps]
    for sent, _ in conv_moves:
        sent.start()
        pending.append(sent)
    conv_in[seq] = conv_out[seq]

    for move in terms_moves:
        move.wait_recv()
    total = terms[pl.ds(dp * group, group)]
    for k in range(dp_count - 1):
        total = total + terms_in[k]
    summed[...] = total
    owned_swap = Swap(lambda i: summed.at[i], lambda slot: owned.at[slot[1]], owned_sem)
    owned_swap.start()

    for _, got in back_moves:
        got.wait_recv()
    grad_input[...] = back_in[...].reshape(rows, positions).astype(jnp.bfloat16)
    for _, got in conv_moves:
        got.wait_recv()
    upstream = out_cot[...].astype(jnp.float32)
    grad_gate[...] = (upstream * conv_in[...].reshape(rows, positions)).astype(jnp.bfloat16)
    owned_swap.wait_recv()
    for i in range(group):
        grad_filter[:, i * own : (i + 1) * own] = owned[i]
    for sent in pending:
        sent.wait_send()
    filt_swap.wait_send()
    owned_swap.wait_send()


def fused(grad_out, gate, input_spectrum, filter_spectrum, tables, dp_count, seq_count):
    _, channels, positions = grad_out.shape
    own = channels // seq_count
    group = seq_count // dp_count
    (cos_hi, cos_lo), (sin_hi, sin_lo), (tw_cos, tw_sin), _ = tables
    vmem = pl.BlockSpec(memory_space=pltpu.VMEM)
    anywhere = pl.BlockSpec(memory_space=pl.ANY)
    single = jnp.float32
    blocks = (seq_count, own, positions)
    pair = lambda count: pltpu.SemaphoreType.DMA((2, count))
    back, gated, filt = pl.pallas_call(
        functools.partial(kernel, dp_count, seq_count, own, min(256, positions)),
        out_shape=(
            jax.ShapeDtypeStruct((channels, positions), jnp.bfloat16),
            jax.ShapeDtypeStruct((channels, positions), jnp.bfloat16),
            jax.ShapeDtypeStruct(filter_spectrum.shape, single),
        ),
        in_specs=[vmem, vmem, anywhere, anywhere, vmem, vmem] + [anywhere] * 4,
        out_specs=(vmem, vmem, vmem),
        scratch_shapes=[
            pltpu.VMEM((4, positions, positions), jnp.bfloat16),
            pltpu.VMEM(blocks, single),
            pltpu.VMEM(blocks, single),
            pltpu.VMEM((2,) + blocks, single),
            pltpu.VMEM((seq_count, 2, own, positions), single),
            pltpu.VMEM((2 * channels, positions), single),
            pltpu.VMEM((4 * channels, positions), jnp.bfloat16),
            pltpu.VMEM((2, channels, positions), single),
            pltpu.VMEM((2, channels, positions), single),
            pltpu.VMEM(blocks, single),
            pltpu.VMEM(blocks, single),
            pltpu.VMEM(blocks, single),
            pltpu.VMEM(blocks, single),
            pltpu.VMEM((seq_count, 2, own, positions), single),
            pltpu.VMEM((dp_count - 1, group, 2, own, positions), single),
            pltpu.VMEM((group, 2, own, positions), single),
            pltpu.VMEM((group, 2, own, positions), single),
            pltpu.SemaphoreType.DMA((4,)),
            pltpu.SemaphoreType.DMA((1,)),
            pair(seq_count),
            pair(seq_count),
            pair(group),
            pair(dp_count),
            pair(seq_count),
            pair(seq_count),
            pair(dp_count),
            pair(group),
        ],
        compiler_params=pltpu.CompilerParams(
            has_side_effects=True, vmem_limit_bytes=48 * 1024 * 1024
        ),
    )(
        grad_out[0], gate[0], input_spectrum[0], filter_spectrum, tw_cos, tw_sin,
        cos_hi, cos_lo, sin_hi, sin_lo,
    )
    return back[None], gated[None], filt


def solution(mesh):
    def per_device(grad_out, gate, input_spectrum, filter_spectrum):
        tables = host_tables(mesh.shape["seq"], grad_out.shape[2])
        batch, channels, positions = grad_out.shape
        dp_count, seq_count = mesh.shape["dp"], mesh.shape["seq"]
        aligned = channels % (8 * seq_count) == 0 and positions % 128 == 0
        if batch == 1 and aligned and seq_count % (2 * dp_count) == 0:
            return fused(
                grad_out, gate, input_spectrum, filter_spectrum, tables, dp_count, seq_count
            )
        return per_device_arrays(grad_out, gate, input_spectrum, filter_spectrum, tables)

    return jax.shard_map(
        per_device,
        mesh=mesh,
        in_specs=(
            P("dp", None, "seq"),
            P("dp", None, "seq"),
            P("dp", None, None, "seq"),
            P(None, "dp", "seq"),
        ),
        out_specs=(P("dp", None, "seq"), P("dp", None, "seq"), P(None, "dp", "seq")),
        check_vma=False,
    )
```

```python
import functools
import math

import jax
import jax.numpy as jnp
import numpy as np
from jax import lax
from jax.experimental import pallas as pl
from jax.experimental.pallas import tpu as pltpu
from jax.sharding import PartitionSpec as P


def host_split(table):
    high = table.astype(jnp.bfloat16)
    low = (table - high.astype(np.float64)).astype(jnp.bfloat16)
    return high, low


def host_tables(seq_count, positions):
    index = np.arange(positions, dtype=np.int64)
    angle = (index[:, None] * index[None, :] % positions) * (2.0 * math.pi / positions)
    total_len = positions * seq_count
    classes = np.arange(seq_count, dtype=np.int64)
    turn = (classes[:, None] * index[None, :] % total_len) * (2.0 * math.pi / total_len)
    small = (classes[:, None] * classes[None, :] % seq_count) * (2.0 * math.pi / seq_count)
    scale = 1.0 / math.sqrt(total_len)
    return (
        host_split(np.cos(angle)),
        host_split(np.sin(angle)),
        ((np.cos(turn) * scale).astype(np.float32), (np.sin(turn) * scale).astype(np.float32)),
        (np.cos(small).astype(np.float32), np.sin(small).astype(np.float32)),
    )


def split_product(values, table):
    high = lax.reduce_precision(values, 8, 7)
    low = (values - high).astype(jnp.bfloat16)
    high = high.astype(jnp.bfloat16)
    rows = values.shape[0]
    both = jnp.dot(
        jnp.concatenate([high, low], axis=0), table[0], preferred_element_type=jnp.float32
    )
    rest = jnp.dot(high, table[1], preferred_element_type=jnp.float32)
    return both[:rows] + both[rows:] + rest


def mixed(matrix, blocks):
    return jnp.einsum(
        "fp,pcq->fcq",
        matrix,
        blocks,
        precision=lax.Precision.HIGHEST,
        preferred_element_type=jnp.float32,
    )


def per_device_arrays(grad_out, gate, input_spectrum, filter_spectrum, tables):
    batch, channels, positions = grad_out.shape
    seq_count = lax.axis_size("seq")
    own = channels // seq_count
    cos_table, sin_table, (tw_cos, tw_sin), (small_cos, small_sin) = tables
    tw_cos = tw_cos[None, :, None, :]
    tw_sin = tw_sin[None, :, None, :]

    def exchange(blocks):
        return lax.all_to_all(blocks, "seq", split_axis=1, concat_axis=1, tiled=True)

    def by_block(array):
        return array.reshape((array.shape[0], seq_count, own, positions))

    def transform(real, imag):
        shape = real.shape
        stacked = jnp.concatenate([real.reshape(-1, positions), imag.reshape(-1, positions)])
        rows = stacked.shape[0] // 2
        by_cos = split_product(stacked, cos_table)
        by_sin = split_product(stacked, sin_table)
        pick = lambda part, half: part[half * rows : (half + 1) * rows].reshape(shape)
        return pick(by_cos, 0), pick(by_cos, 1), pick(by_sin, 0), pick(by_sin, 1)

    def inverse(real, imag):
        rc, ic, rs, is_ = transform(real, imag)
        local_real, local_imag = rc - is_, ic + rs
        turned_real = local_real * tw_cos - local_imag * tw_sin
        turned_imag = local_imag * tw_cos + local_real * tw_sin
        return jax.vmap(
            lambda a, b: mixed(small_cos, a) - mixed(small_sin, b)
        )(turned_real, turned_imag)

    upstream = grad_out.astype(jnp.float32)
    delta = by_block(exchange(upstream * gate.astype(jnp.float32)))
    filters = lax.all_gather(filter_spectrum, "dp", axis=1, tiled=True)
    spectra = exchange(
        jnp.concatenate([input_spectrum.reshape((-1,) + input_spectrum.shape[2:]), filters])
    )
    spectra = by_block(spectra)
    in_real, in_imag = spectra[0 : 2 * batch : 2], spectra[1 : 2 * batch : 2]
    filt_real, filt_imag = spectra[2 * batch], spectra[2 * batch + 1]

    part_real = jax.vmap(lambda a: mixed(small_cos, a))(delta)
    part_imag = -jax.vmap(lambda a: mixed(small_sin, a))(delta)
    turned_real = part_real * tw_cos + part_imag * tw_sin
    turned_imag = part_imag * tw_cos - part_real * tw_sin
    rc, ic, rs, is_ = transform(turned_real, turned_imag)
    delta_real, delta_imag = rc + is_, ic - rs

    conv = inverse(
        in_real * filt_real - in_imag * filt_imag, in_real * filt_imag + in_imag * filt_real
    )
    backward = inverse(
        filt_real * delta_real + filt_imag * delta_imag,
        filt_real * delta_imag - filt_imag * delta_real,
    )
    term_real = jnp.sum(in_real * delta_real + in_imag * delta_imag, axis=0)
    term_imag = jnp.sum(in_real * delta_imag - in_imag * delta_real, axis=0)
    results = jnp.concatenate([conv, backward, jnp.stack([term_real, term_imag])])
    results = exchange(results.reshape(-1, channels, positions))
    conv, backward, terms = (
        results[:batch],
        results[batch : 2 * batch],
        results[2 * batch :],
    )
    grad_filter = lax.psum_scatter(terms, "dp", scatter_dimension=1, tiled=True)
    conv, backward = lax.optimization_barrier((conv, backward))
    return (
        backward.astype(jnp.bfloat16),
        (upstream * conv).astype(jnp.bfloat16),
        grad_filter,
    )


MESH = pl.DeviceIdType.MESH


def weighted(terms):
    total = None
    for weight, value in terms:
        if abs(weight) < 1e-12:
            continue
        if abs(abs(weight) - 1.0) < 1e-12:
            if total is None:
                total = value if weight > 0 else -value
            else:
                total = total + value if weight > 0 else total - value
        else:
            total = value * weight if total is None else total + value * weight
    return total


def kernel(
    dp_count, seq_count, own, tile,
    cot_home, gate_home, spectrum, filt, cos_home, sin_home, cos_hi, cos_lo, sin_hi, sin_lo,
    grad_input, grad_gate, grad_filter,
    out_cot, gate, tw_cos, tw_sin, tables, delta_out, delta_in, spec_in, filt_in, staged, split, spec_delta, local,
    back_out, back_in, conv_out, conv_in, terms, terms_in, summed, owned,
    table_sem, self_sem, delta_sem, spec_sem, filt_sem, spread_sem,
    back_sem, conv_sem, terms_sem, owned_sem,
):
    dp = lax.axis_index("dp")
    seq = lax.axis_index("seq")
    group = seq_count // dp_count
    positions = cot_home.shape[1]
    rows = seq_count * own
    home, place = seq // group, seq % group

    table_copies = [
        pltpu.make_async_copy(src, tables.at[i], table_sem.at[i])
        for i, src in enumerate((cos_hi, sin_hi, cos_lo, sin_lo))
    ]

    early = [
        pltpu.make_async_copy(src, dst, self_sem.at[1 + i])
        for i, (src, dst) in enumerate(
            ((cot_home, out_cot), (gate_home, gate), (cos_home, tw_cos), (sin_home, tw_sin))
        )
    ]
    for copy in early:
        copy.start()
    barrier = pltpu.get_barrier_semaphore()

    def greet(dp_to, seq_to):
        pl.semaphore_signal(
            barrier, inc=1, device_id={"dp": dp_to, "seq": seq_to}, device_id_type=MESH
        )

    for k in range(1, seq_count):
        greet(dp, lax.rem(seq + k, seq_count))
    for k in range(1, dp_count):
        greet(lax.rem(dp + k, dp_count), seq)
    among = jnp.int32(0)
    for i in range(group):
        own_part = (dp == home) & (place == i)
        pl.when(jnp.logical_not(own_part))(functools.partial(greet, home, dp * group + i))
        among = among + own_part.astype(jnp.int32)
    for copy in early:
        copy.wait()
    upstream = out_cot[...].astype(jnp.float32)
    delta_out[...] = (upstream * gate[...].astype(jnp.float32)).reshape(delta_out.shape)
    pl.semaphore_wait(barrier, seq_count - 1 + dp_count - 1 + group - among)

    def seq_peer(step):
        return lax.rem(seq + step, seq_count)

    def seq_exchange(source_of, target_of, sems, step):
        to, come = seq_peer(step), seq_peer(seq_count - step)
        make = lambda source, target: pltpu.make_async_remote_copy(
            src_ref=source_of(source), dst_ref=target_of(target),
            send_sem=sems.at[0, step], recv_sem=sems.at[1, step],
            device_id={"dp": dp, "seq": to}, device_id_type=MESH,
        )
        return make(to, seq), make(to, come)

    def dp_exchange(source_of, target_of, sems, step):
        to, come = lax.rem(dp + step, dp_count), lax.rem(dp + dp_count - step, dp_count)
        make = lambda source, target: pltpu.make_async_remote_copy(
            src_ref=source_of(source), dst_ref=target_of(target),
            send_sem=sems.at[0, step], recv_sem=sems.at[1, step],
            device_id={"dp": to, "seq": seq}, device_id_type=MESH,
        )
        return make(to, dp), make(to, come)

    class Swap:
        def __init__(self, source_of, target_of, sems):
            self.parts = []
            for i in range(group):
                own_part = (dp == home) & (place == i)
                make = lambda slot, i=i: pltpu.make_async_remote_copy(
                    src_ref=source_of(i), dst_ref=target_of(slot),
                    send_sem=sems.at[0, i], recv_sem=sems.at[1, slot[1]],
                    device_id={"dp": home, "seq": dp * group + i}, device_id_type=MESH,
                )
                here = pltpu.make_async_copy(
                    source_of(i), target_of((seq, place)), sems.at[0, i]
                )
                self.parts.append(
                    (own_part, make((seq, place)), make((dp * group + i, i)), here)
                )

        def start(self):
            for own_part, sent, _, here in self.parts:
                pl.when(own_part)(here.start)
                pl.when(jnp.logical_not(own_part))(sent.start)

        def wait_recv(self):
            for own_part, _, got, here in self.parts:
                pl.when(own_part)(here.wait)
                pl.when(jnp.logical_not(own_part))(got.wait_recv)

        def wait_send(self):
            for own_part, sent, _, _ in self.parts:
                pl.when(jnp.logical_not(own_part))(sent.wait_send)

    steps = range(1, seq_count)
    pending = []

    delta_moves = [seq_exchange(lambda b: delta_out.at[b], lambda b: delta_in.at[b], delta_sem, k) for k in steps]
    for sent, _ in delta_moves:
        sent.start()
        pending.append(sent)
    filt_swap = Swap(
        lambda i: filt.at[:, pl.ds(i * own, own), :],
        lambda slot: filt_in.at[slot[0]],
        filt_sem,
    )
    filt_swap.start()
    block = lambda b: spectrum.at[:, pl.ds(pl.multiple_of(b * own, own), own), :]
    spec_moves = [seq_exchange(block, lambda b: spec_in.at[:, b], spec_sem, k) for k in steps]
    spec_here = pltpu.make_async_copy(block(seq), spec_in.at[:, seq], self_sem.at[0])
    spec_here.start()
    for copy in table_copies:
        copy.start()
    delta_in[seq] = delta_out[seq]
    for _, got in delta_moves:
        got.wait_recv()

    for sent, _ in spec_moves:
        sent.start()
        pending.append(sent)
    filt_swap.wait_recv()
    mine = lambda _: filt_in.at[pl.ds(dp * group, group)]
    spread = []
    for k in range(1, dp_count):
        sent, _ = dp_exchange(mine, mine, spread_sem, k)
        come = lax.rem(dp + dp_count - k, dp_count)
        _, got = dp_exchange(mine, lambda _, come=come: filt_in.at[pl.ds(come * group, group)], spread_sem, k)
        sent.start()
        pending.append(sent)
        spread.append(got)

    half = seq_count // 2
    angle = 2.0 * math.pi / seq_count

    def cos_of(n):
        return math.cos(angle * (n % seq_count))

    def sin_of(n):
        return math.sin(angle * (n % seq_count))

    def put(freq, real, imag):
        staged[freq * own : (freq + 1) * own] = real
        staged[rows + freq * own : rows + (freq + 1) * own] = imag

    def transform(target, sign):
        values = staged[...]
        high = values.astype(jnp.bfloat16)
        split[: 2 * rows] = high
        split[2 * rows :] = (values - high.astype(jnp.float32)).astype(jnp.bfloat16)

        def one(j, carry):
            columns = pl.ds(pl.multiple_of(j * tile, tile), tile)

            def product(high_at, low_at):
                both = jnp.dot(split[...], tables[high_at, :, columns], preferred_element_type=jnp.float32)
                rest = jnp.dot(split[: 2 * rows], tables[low_at, :, columns], preferred_element_type=jnp.float32)
                return both[: 2 * rows] + both[2 * rows :] + rest

            by_cos = product(0, 2)
            by_sin = product(1, 3)
            if sign > 0:
                target[0, :, columns] = by_cos[:rows] - by_sin[rows:]
                target[1, :, columns] = by_cos[rows:] + by_sin[:rows]
            else:
                target[0, :, columns] = by_cos[:rows] + by_sin[rows:]
                target[1, :, columns] = by_cos[rows:] - by_sin[:rows]
            return carry

        lax.fori_loop(0, positions // tile, one, 0)

    def inverse(target):
        transform(local, 1)
        real, imag = [], []
        for f in range(seq_count):
            a = local[0, f * own : (f + 1) * own]
            b = local[1, f * own : (f + 1) * own]
            c, s = tw_cos[f : f + 1], tw_sin[f : f + 1]
            real.append(a * c - b * s)
            imag.append(b * c + a * s)
        pairs = [
            (f, real[f] + real[seq_count - f], imag[f] - imag[seq_count - f])
            for f in range(1, half)
        ]
        for p in range(seq_count):
            parts = [(1.0, real[0]), (cos_of(p * half), real[half])]
            for f, a, b in pairs:
                parts += [(cos_of(p * f), a), (-sin_of(p * f), b)]
            target[p] = weighted(parts)

    blocks = [delta_in[p] for p in range(seq_count)]
    for f in range(half + 1):
        real = weighted([(cos_of(p * f), blocks[p]) for p in range(seq_count)])
        imag = weighted([(-sin_of(p * f), blocks[p]) for p in range(seq_count)])
        for g, turn in {f: 1.0, (seq_count - f) % seq_count: -1.0 if f % half else 1.0}.items():
            c, s = tw_cos[g : g + 1], tw_sin[g : g + 1]
            if imag is None:
                put(g, real * c, -(real * s))
            else:
                b = imag if turn > 0 else -imag
                put(g, real * c + b * s, b * c - real * s)
    for copy in table_copies:
        copy.wait()
    transform(spec_delta, -1)

    for got in spread:
        got.wait_recv()
    for f in range(seq_count):
        a, b = filt_in[f, 0], filt_in[f, 1]
        c = spec_delta[0, f * own : (f + 1) * own]
        d = spec_delta[1, f * own : (f + 1) * own]
        put(f, a * c + b * d, a * d - b * c)
    inverse(back_out)
    back_moves = [seq_exchange(lambda b: back_out.at[b], lambda b: back_in.at[b], back_sem, k) for k in steps]
    for sent, _ in back_moves:
        sent.start()
        pending.append(sent)
    back_in[seq] = back_out[seq]

    spec_here.wait()
    for _, got in spec_moves:
        got.wait_recv()
    for f in range(seq_count):
        a, b = spec_in[0, f], spec_in[1, f]
        c = spec_delta[0, f * own : (f + 1) * own]
        d = spec_delta[1, f * own : (f + 1) * own]
        terms[f, 0] = a * c + b * d
        terms[f, 1] = a * d - b * c
        c, d = filt_in[f, 0], filt_in[f, 1]
        put(f, a * c - b * d, a * d + b * c)
    quarter = lambda h: terms.at[pl.ds(h * group, group)]
    terms_moves = []
    for k in range(1, dp_count):
        sent, _ = dp_exchange(quarter, lambda _, k=k: terms_in.at[k - 1], terms_sem, k)
        sent.start()
        pending.append(sent)
        terms_moves.append(sent)
    inverse(conv_out)
    conv_moves = [seq_exchange(lambda b: conv_out.at[b], lambda b: conv_in.at[b], conv_sem, k) for k in steps]
    for sent, _ in conv_moves:
        sent.start()
        pending.append(sent)
    conv_in[seq] = conv_out[seq]

    for move in terms_moves:
        move.wait_recv()
    total = terms[pl.ds(dp * group, group)]
    for k in range(dp_count - 1):
        total = total + terms_in[k]
    summed[...] = total
    owned_swap = Swap(lambda i: summed.at[i], lambda slot: owned.at[slot[1]], owned_sem)
    owned_swap.start()

    for _, got in back_moves:
        got.wait_recv()
    grad_input[...] = back_in[...].reshape(rows, positions).astype(jnp.bfloat16)
    for _, got in conv_moves:
        got.wait_recv()
    upstream = out_cot[...].astype(jnp.float32)
    grad_gate[...] = (upstream * conv_in[...].reshape(rows, positions)).astype(jnp.bfloat16)
    owned_swap.wait_recv()
    for i in range(group):
        grad_filter[:, i * own : (i + 1) * own] = owned[i]
    for sent in pending:
        sent.wait_send()
    filt_swap.wait_send()
    owned_swap.wait_send()


def fused(grad_out, gate, input_spectrum, filter_spectrum, tables, dp_count, seq_count):
    _, channels, positions = grad_out.shape
    own = channels // seq_count
    group = seq_count // dp_count
    (cos_hi, cos_lo), (sin_hi, sin_lo), (tw_cos, tw_sin), _ = tables
    vmem = pl.BlockSpec(memory_space=pltpu.VMEM)
    far = pl.BlockSpec(memory_space=pltpu.HBM)
    single = jnp.float32
    blocks = (seq_count, own, positions)
    pair = lambda count: pltpu.SemaphoreType.DMA((2, count))
    back, gated, filt = pl.pallas_call(
        functools.partial(kernel, dp_count, seq_count, own, min(256, positions)),
        out_shape=(
            jax.ShapeDtypeStruct((channels, positions), jnp.bfloat16),
            jax.ShapeDtypeStruct((channels, positions), jnp.bfloat16),
            jax.ShapeDtypeStruct(filter_spectrum.shape, single),
        ),
        in_specs=[far] * 10,
        out_specs=(vmem, vmem, vmem),
        scratch_shapes=[
            pltpu.VMEM((channels, positions), jnp.bfloat16),
            pltpu.VMEM((channels, positions), jnp.bfloat16),
            pltpu.VMEM((seq_count, positions), single),
            pltpu.VMEM((seq_count, positions), single),
            pltpu.VMEM((4, positions, positions), jnp.bfloat16),
            pltpu.VMEM(blocks, single),
            pltpu.VMEM(blocks, single),
            pltpu.VMEM((2,) + blocks, single),
            pltpu.VMEM((seq_count, 2, own, positions), single),
            pltpu.VMEM((2 * channels, positions), single),
            pltpu.VMEM((4 * channels, positions), jnp.bfloat16),
            pltpu.VMEM((2, channels, positions), single),
            pltpu.VMEM((2, channels, positions), single),
            pltpu.VMEM(blocks, single),
            pltpu.VMEM(blocks, single),
            pltpu.VMEM(blocks, single),
            pltpu.VMEM(blocks, single),
            pltpu.VMEM((seq_count, 2, own, positions), single),
            pltpu.VMEM((dp_count - 1, group, 2, own, positions), single),
            pltpu.VMEM((group, 2, own, positions), single),
            pltpu.VMEM((group, 2, own, positions), single),
            pltpu.SemaphoreType.DMA((4,)),
            pltpu.SemaphoreType.DMA((5,)),
            pair(seq_count),
            pair(seq_count),
            pair(group),
            pair(dp_count),
            pair(seq_count),
            pair(seq_count),
            pair(dp_count),
            pair(group),
        ],
        compiler_params=pltpu.CompilerParams(
            collective_id=0, has_side_effects=True, vmem_limit_bytes=56 * 1024 * 1024
        ),
    )(
        grad_out[0], gate[0], input_spectrum[0], filter_spectrum, tw_cos, tw_sin,
        cos_hi, cos_lo, sin_hi, sin_lo,
    )
    return back[None], gated[None], filt


def solution(mesh):
    def per_device(grad_out, gate, input_spectrum, filter_spectrum):
        tables = host_tables(mesh.shape["seq"], grad_out.shape[2])
        batch, channels, positions = grad_out.shape
        dp_count, seq_count = mesh.shape["dp"], mesh.shape["seq"]
        aligned = channels % (8 * seq_count) == 0 and positions % 128 == 0
        if batch == 1 and aligned and seq_count % (2 * dp_count) == 0:
            return fused(
                grad_out, gate, input_spectrum, filter_spectrum, tables, dp_count, seq_count
            )
        return per_device_arrays(grad_out, gate, input_spectrum, filter_spectrum, tables)

    return jax.shard_map(
        per_device,
        mesh=mesh,
        in_specs=(
            P("dp", None, "seq"),
            P("dp", None, "seq"),
            P("dp", None, None, "seq"),
            P(None, "dp", "seq"),
        ),
        out_specs=(P("dp", None, "seq"), P("dp", None, "seq"), P(None, "dp", "seq")),
        check_vma=False,
    )
```
